256 devices in a mesh: tm: 8 (over z), chan: 32 (over x, y, core).
Axes of the slice: x: 4, y: 4, z: 8, core: 2. Of those that a mesh axis runs over, the one named last changes fastest.
Arguments:
- voltages: bfloat16 [512, 1024, 2048], P('chan', None, 'tm'), may hold values from -4 to 4
- exponents: int32 [512, 16, 8], P('chan', None, 'tm'), may hold values from -2 to 2
- gain_real: float32 [512, 1024], P(None, 'chan'), may hold values from 0.1 to 1.9
- gain_imag: float32 [512, 1024], P(None, 'chan'), may hold values from -1.5 to 1.5
- delays: float32 [512, 256], replicated, may hold values from -8 to 8
- filter_taps: float32 [4, 1024], replicated, may hold values from -3 to 3
Outputs:
- beam_series: bfloat16 [256, 1024, 2048], P('chan', None, 'tm')
The draws below stay inside these ranges and needn't reach their ends.
All inputs are finite; a program needn't handle non-finite values.
Results may differ from the reference program's by a relative error of at most 0.0062.
Values may be sent and summed in bfloat16 or wider, within the bound.
No kernel may reach another device: no remote copies, remote signals or barrier semaphores. Data moves between devices by JAX's collectives and lax.ppermute only.
A program may use at most 128 MiB of HBM per device.

```python
import math
import jax
import jax.numpy as jnp
from jax import lax

S = 512
C = 1024
B = 256
TAPS = 4
CB = 64
F_DEV = 128
GROUPS = 8
NF = 1024
SCALE_BLOCKS = 16
N_TM = 8


def set_ends(result, rng, low, high):
    spot = [jax.random.randint(jax.random.fold_in(rng, axis), (), 0, length) for axis, length in enumerate(result.shape)]
    longest = result.shape.index(max(result.shape))
    next_to = spot[:longest] + [(spot[longest] + 1) % result.shape[longest]] + spot[longest + 1:]
    return result.at[tuple(spot)].set(low).at[tuple(next_to)].set(high)


def steps_of(rng, dims, cuts, low, top_value):
    loudness, own = 1.0, jax.random.fold_in(rng, 6)
    for dim, shards_of in cuts:
        heights = jnp.exp(jax.random.uniform(jax.random.fold_in(own, dim), (shards_of,), jnp.float32, low / len(cuts), top_value / len(cuts)))
        loudness = loudness * jnp.repeat(heights, dims[dim] // shards_of).reshape([-1 if axis == dim else 1 for axis in range(len(dims))])
    return loudness


def scatter_about(rng, dims, deviation, bound, split=(), kind=jnp.bfloat16):
    drawn = deviation * jax.random.normal(rng, dims, jnp.float32)
    if split:
        drawn = drawn * steps_of(rng, dims, split, -0.22, 0.18)
    return jnp.clip(drawn, -bound, bound).astype(kind)


def setup_inputs(seed: int = 0) -> dict:
    seeds = jax.random.split(jax.random.key(seed), 7)
    return {
        "voltages": scatter_about(seeds[0], (S, C, 2 * NF), 1.0, 4.0, ((0, 32), (2, 8))),
        "exponents": set_ends(jax.random.randint(seeds[1], (S, SCALE_BLOCKS, GROUPS), -2, 3), jax.random.fold_in(seeds[1], 1), -2, 2).astype(jnp.int32),
        "gain_real": jnp.clip(1.0 + 0.18 * jax.random.normal(seeds[2], (S, C), jnp.float32), 0.1, 1.9),
        "gain_imag": scatter_about(seeds[3], (S, C), 0.3, 1.5, ((1, 32),), jnp.float32),
        "delays": jnp.clip(jax.random.uniform(seeds[4], (S, B), jnp.float32, -8.0, 8.0), -8.0, 8.0),
        "filter_taps": scatter_about(seeds[5], (TAPS, C), 0.5, 3.0, (), jnp.float32),
    }


TWO_PI = 6.283185307179586

def inverse_tables(length):
    row_index = lax.broadcasted_iota(jnp.int32, (length, length), 0)
    col_index = lax.broadcasted_iota(jnp.int32, (length, length), 1)
    phases = TWO_PI / length * (row_index * col_index % length).astype(jnp.float32)
    normalizer = 1.0 / math.sqrt(length)
    cosine_table = (jnp.cos(phases) * normalizer).astype(jnp.bfloat16)
    sine_table = (jnp.sin(phases) * normalizer).astype(jnp.bfloat16)
    return (cosine_table, sine_table)

def reference(voltages, exponents, gain_real, gain_imag, delays, filter_taps):
    stations = voltages.shape[0]
    beam_count = delays.shape[1]
    scale_factor = 1.0 / math.sqrt(stations)
    cosine_table, sine_table = inverse_tables(C)

    def one_channel(channel_index):
        samples = lax.dynamic_index_in_dim(voltages, channel_index, 1, keepdims=False)
        exponent_row = lax.dynamic_index_in_dim(exponents, channel_index // CB, 1, keepdims=False)
        factor = jnp.exp2(exponent_row.astype(jnp.float32)).astype(jnp.bfloat16)
        scaled = (samples.reshape(stations, N_TM, 2 * F_DEV) * factor[:, :, None]).reshape(stations, 2 * NF)
        frequency = (channel_index.astype(jnp.float32) + 0.5) / C - 0.5
        phases = TWO_PI * frequency * jnp.transpose(delays)
        cosines = jnp.cos(phases)
        sines = jnp.sin(phases)
        real_gain = lax.dynamic_index_in_dim(gain_real, channel_index, 1, keepdims=False)[None, :]
        imag_gain = lax.dynamic_index_in_dim(gain_imag, channel_index, 1, keepdims=False)[None, :]
        weight_real = (real_gain * cosines + imag_gain * sines) * scale_factor
        weight_imag = (imag_gain * cosines - real_gain * sines) * scale_factor
        weights = jnp.concatenate([weight_real, weight_imag], axis=0).astype(jnp.bfloat16)
        product = jnp.dot(weights, scaled, preferred_element_type=jnp.float32).reshape(2 * beam_count, N_TM, 2, F_DEV)
        real_part = product[:beam_count, :, 0] - product[beam_count:, :, 1]
        imag_part = product[:beam_count, :, 1] + product[beam_count:, :, 0]
        return jnp.stack([real_part, imag_part], axis=2).astype(jnp.bfloat16)
    beams = lax.map(one_channel, jnp.arange(C, dtype=jnp.int32))
    tail_length = filter_taps.shape[0] - 1

    def one_beam(beam_index):
        spectra = lax.dynamic_index_in_dim(beams, beam_index, 1, keepdims=False).reshape(C, 2 * NF)
        cosine_part = jnp.dot(jnp.transpose(cosine_table), spectra, preferred_element_type=jnp.float32).reshape(C, N_TM, 2, F_DEV)
        sine_part = jnp.dot(jnp.transpose(sine_table), spectra, preferred_element_type=jnp.float32).reshape(C, N_TM, 2, F_DEV)
        real_part = cosine_part[:, :, 0] - sine_part[:, :, 1]
        imag_part = sine_part[:, :, 0] + cosine_part[:, :, 1]
        signal = jnp.stack([real_part, imag_part], axis=1).reshape(C, 2, NF)
        extended = jnp.concatenate([jnp.zeros((C, 2, tail_length), jnp.float32), signal], axis=2)
        running = jnp.zeros((C, 2, NF), jnp.float32)
        for tap_index in range(filter_taps.shape[0]):
            begin = tail_length - tap_index
            running = running + filter_taps[tap_index][:, None, None] * extended[:, :, begin:begin + NF]
        packed = jnp.transpose(running.reshape(C, 2, N_TM, F_DEV), (0, 2, 1, 3)).reshape(C, 2 * NF)
        return packed.astype(jnp.bfloat16)
    return lax.map(one_beam, jnp.arange(beam_count, dtype=jnp.int32))
```

```python
import math

import jax
import jax.numpy as jnp
from jax import lax
from jax.experimental import pallas as pl
from jax.experimental.pallas import tpu as pltpu
from jax.sharding import PartitionSpec as P

C = 1024
TAPS = 4
TILE = 16
FR = 128
TWO_PI = 6.283185307179586


def swap_matrix():
    row = lax.broadcasted_iota(jnp.int32, (256, 256), 0)
    col = lax.broadcasted_iota(jnp.int32, (256, 256), 1)
    hit = (row // TILE == col % TILE) & (row % TILE == col // TILE)
    return jnp.where(hit, 1.0, 0.0).astype(jnp.bfloat16)


def parity_table(parity):
    sample = lax.broadcasted_iota(jnp.int32, (C // 2, C // 2), 0)
    channel = 2 * lax.broadcasted_iota(jnp.int32, (C // 2, C // 2), 1) + parity
    phases = TWO_PI / C * (sample * channel % C).astype(jnp.float32)
    normalizer = 1.0 / math.sqrt(C)
    cosines = (jnp.cos(phases) * normalizer).astype(jnp.bfloat16)
    sines = (jnp.sin(phases) * normalizer).astype(jnp.bfloat16)
    return jnp.concatenate([cosines, sines], axis=0)


def beam_weights(gain_real, gain_imag, delays, chan_start):
    local_count = gain_real.shape[1]
    stations = delays.shape[0]
    channel = (chan_start + lax.broadcasted_iota(jnp.int32, (local_count,), 0)).astype(jnp.float32)
    frequency = (channel + 0.5) / C - 0.5
    turns = TWO_PI * frequency
    phases = turns[:, None, None] * jnp.transpose(delays)[None, :, :]
    cosines = jnp.cos(phases)
    sines = jnp.sin(phases)
    real_gain = jnp.transpose(gain_real)[:, None, :]
    imag_gain = jnp.transpose(gain_imag)[:, None, :]
    scale_factor = 1.0 / math.sqrt(stations)
    weight_real = (real_gain * cosines + imag_gain * sines) * scale_factor
    weight_imag = (imag_gain * cosines - real_gain * sines) * scale_factor
    return weight_real.astype(jnp.bfloat16), weight_imag.astype(jnp.bfloat16)


SC_STEP = 128
CB = 64


def scale_kernel(exp_ref, volt_ref, out_ref, perm_ref):
    step = pl.program_id(0)

    @pl.when(step == 0)
    def _():
        perm_ref[...] = swap_matrix()

    station = lax.broadcasted_iota(jnp.int32, (TILE, 2 * FR), 0)
    for block in range(SC_STEP // CB):
        power = jnp.zeros((TILE, 2 * FR), jnp.int32)
        for s in range(TILE):
            power = jnp.where(station == s, exp_ref[s, step * (SC_STEP // CB) + block], power)
        factor = jnp.exp2(power.astype(jnp.float32)).astype(jnp.bfloat16).astype(jnp.float32)
        for part in range(CB // TILE):
            start = block * CB + part * TILE
            rows = volt_ref[:, start : start + TILE, :].reshape(256, 2 * FR)
            moved = jnp.dot(perm_ref[...], rows, preferred_element_type=jnp.float32)
            scaled = moved.reshape(TILE, TILE, 2 * FR) * factor[None]
            out_ref[start : start + TILE] = scaled.astype(jnp.bfloat16)


def scale_and_turn(voltages, exponents):
    return pl.pallas_call(
        scale_kernel,
        grid=(C // SC_STEP,),
        in_specs=[
            pl.BlockSpec(memory_space=pltpu.SMEM),
            pl.BlockSpec((TILE, SC_STEP, 2 * FR), lambda i: (0, i, 0)),
        ],
        out_specs=pl.BlockSpec((SC_STEP, TILE, 2 * FR), lambda i: (i, 0, 0)),
        out_shape=jax.ShapeDtypeStruct((C, TILE, 2 * FR), jnp.bfloat16),
        scratch_shapes=[pltpu.VMEM((256, 256), jnp.bfloat16)],
        compiler_params=pltpu.CompilerParams(vmem_limit_bytes=24 * 2**20),
        name="scale",
    )(exponents, voltages)


BF_STEP = 2


def beam_kernel(wr_ref, wi_ref, x_ref, out_ref, perm_ref, beams_ref):
    q, j = pl.program_id(0), pl.program_id(1)

    @pl.when((q == 0) & (j == 0))
    def _():
        perm_ref[...] = swap_matrix()

    for i in range(BF_STEP):
        x = x_ref[:, i, 0].reshape(512, 2 * FR)
        pr = jnp.dot(wr_ref[i, 0], x, preferred_element_type=jnp.float32)
        pi = jnp.dot(wi_ref[i, 0], x, preferred_element_type=jnp.float32)
        real = pr[:, :FR] - pi[:, FR:]
        imag = pr[:, FR:] + pi[:, :FR]
        beams_ref[j * BF_STEP + i, :, :FR] = real.astype(jnp.bfloat16)
        beams_ref[j * BF_STEP + i, :, FR:] = imag.astype(jnp.bfloat16)

    @pl.when(j == pl.num_programs(1) - 1)
    def _():
        for group in range(256 // TILE):
            rows = beams_ref[:, group * TILE : (group + 1) * TILE, :].reshape(256, 2 * FR)
            moved = jnp.dot(perm_ref[...], rows, preferred_element_type=jnp.float32)
            out_ref[group * TILE : (group + 1) * TILE, 0] = moved.reshape(
                TILE, TILE, 2 * FR
            ).astype(jnp.bfloat16)


def form_beams(weight_real, weight_imag, received):
    weight_spec = pl.BlockSpec((BF_STEP, 1, 256, 512), lambda q, j: (j, q, 0, 0))
    return pl.pallas_call(
        beam_kernel,
        grid=(2, 16 // BF_STEP),
        in_specs=[
            weight_spec,
            weight_spec,
            pl.BlockSpec((32, BF_STEP, 1, TILE, 2 * FR), lambda q, j: (0, j, q, 0, 0)),
        ],
        out_specs=pl.BlockSpec((256, 1, TILE, 2 * FR), lambda q, j: (0, q, 0, 0)),
        out_shape=jax.ShapeDtypeStruct((256, 2, TILE, 2 * FR), jnp.bfloat16),
        scratch_shapes=[
            pltpu.VMEM((256, 256), jnp.bfloat16),
            pltpu.VMEM((16, 256, 2 * FR), jnp.bfloat16),
        ],
        compiler_params=pltpu.CompilerParams(vmem_limit_bytes=32 * 2**20),
        name="beamform",
    )(
        weight_real.reshape(16, 2, 256, 512),
        weight_imag.reshape(16, 2, 256, 512),
        received.reshape(32, 16, 2, TILE, 2 * FR),
    )


HALF = C // 2
ROWS = 64


def synth_kernel(te_ref, to_ref, taps_ref, ptaps_ref, y_ref, out_ref, tail_ref, even_ref, odd_ref, pack_ref):
    beam = pl.program_id(0)
    even = y_ref[:, 0, 0].reshape(HALF, 2 * FR)
    odd = y_ref[:, 0, 1].reshape(HALF, 2 * FR)
    even_ref[...] = jnp.dot(te_ref[...], even, preferred_element_type=jnp.float32)
    odd_ref[...] = jnp.dot(to_ref[...], odd, preferred_element_type=jnp.float32)
    lane = lax.broadcasted_iota(jnp.int32, (ROWS, FR), 1)
    slot = lane // 4
    for r in range(0, HALF, ROWS):
        cos_rows, sin_rows = pl.ds(r, ROWS), pl.ds(HALF + r, ROWS)
        parts = []
        for ref in (even_ref, odd_ref):
            real = ref[cos_rows, :FR] - ref[sin_rows, FR:]
            imag = ref[sin_rows, :FR] + ref[cos_rows, FR:]
            parts.append((real, imag))
        packed = pack_ref[cos_rows, :]
        for n1 in range(2):
            for ri in range(2):
                a, b = parts[0][ri], parts[1][ri]
                signal = a + b if n1 == 0 else a - b
                total = taps_ref[0, pl.ds(n1 * HALF + r, ROWS), :] * signal
                for k in range(1, TAPS):
                    shifted = jnp.where(lane >= k, pltpu.roll(signal, k, 1), 0.0)
                    total += taps_ref[k, pl.ds(n1 * HALF + r, ROWS), :] * shifted
                out_ref[0, pl.ds(n1 * HALF + r, ROWS), ri * FR : (ri + 1) * FR] = total.astype(
                    jnp.bfloat16
                )
                where = beam * 4 + n1 * 2 + ri
                packed = jnp.where(slot == where, pltpu.roll(signal, (where * 4 + 4) % FR, 1), packed)
        pack_ref[cos_rows, :] = packed

    @pl.when(beam == pl.num_programs(0) - 1)
    def _():
        for r in range(0, HALF, ROWS):
            rows = pl.ds(r, ROWS)
            packed = pack_ref[rows, :]
            total = jnp.zeros((ROWS, FR), jnp.float32)
            for k in range(1, TAPS):
                moved = jnp.where(lane % 4 < k, pltpu.roll(packed, FR - (4 - k), 1), 0.0)
                total += ptaps_ref[k - 1, rows, :] * moved
            tail_ref[rows, :] = total.astype(jnp.bfloat16)


def synthesize(table_even, table_odd, wide_taps, packed_taps, received):
    whole = pl.BlockSpec(memory_space=pltpu.VMEM)
    return pl.pallas_call(
        synth_kernel,
        grid=(8,),
        in_specs=[
            whole,
            whole,
            whole,
            whole,
            pl.BlockSpec((32, 1, 2, TILE, 2 * FR), lambda b: (0, b, 0, 0, 0)),
        ],
        out_specs=[
            pl.BlockSpec((1, C, 2 * FR), lambda b: (b, 0, 0)),
            pl.BlockSpec((HALF, FR), lambda b: (0, 0)),
        ],
        out_shape=[
            jax.ShapeDtypeStruct((8, C, 2 * FR), jnp.bfloat16),
            jax.ShapeDtypeStruct((HALF, FR), jnp.bfloat16),
        ],
        scratch_shapes=[
            pltpu.VMEM((C, 2 * FR), jnp.float32),
            pltpu.VMEM((C, 2 * FR), jnp.float32),
            pltpu.VMEM((HALF, FR), jnp.float32),
        ],
        compiler_params=pltpu.CompilerParams(vmem_limit_bytes=32 * 2**20),
        name="synthesis",
    )(table_even, table_odd, wide_taps, packed_taps, received)


def patch_kernel(in_ref, series_ref, out_ref):
    beam = pl.program_id(0)
    lane = lax.broadcasted_iota(jnp.int32, (ROWS, FR), 1)
    for r in range(0, HALF, ROWS):
        incoming = in_ref[pl.ds(r, ROWS), :].astype(jnp.float32)
        for n1 in range(2):
            for ri in range(2):
                where = beam * 4 + n1 * 2 + ri
                head = jnp.where(lane < TAPS - 1, pltpu.roll(incoming, (FR - where * 4) % FR, 1), 0.0)
                rows, cols = pl.ds(n1 * HALF + r, ROWS), slice(ri * FR, (ri + 1) * FR)
                old = series_ref[0, rows, cols].astype(jnp.float32)
                out_ref[0, rows, cols] = (old + head).astype(jnp.bfloat16)


def patch(incoming, series):
    block = pl.BlockSpec((1, C, 2 * FR), lambda b: (b, 0, 0))
    return pl.pallas_call(
        patch_kernel,
        grid=(8,),
        in_specs=[
            pl.BlockSpec(memory_space=pltpu.VMEM),
            block,
        ],
        out_specs=block,
        out_shape=jax.ShapeDtypeStruct((8, C, 2 * FR), jnp.bfloat16),
        input_output_aliases={1: 0},
        compiler_params=pltpu.CompilerParams(vmem_limit_bytes=16 * 2**20),
        name="patch",
    )(incoming, series)


def per_device(voltages, exponents, gain_real, gain_imag, delays, filter_taps):
    local_count = gain_real.shape[1]
    turned = scale_and_turn(voltages, exponents.reshape(TILE, -1))
    received = lax.all_to_all(turned, "chan", split_axis=0, concat_axis=0, tiled=True)
    weight_real, weight_imag = beam_weights(
        gain_real, gain_imag, delays, lax.axis_index("chan") * local_count
    )
    beamed = form_beams(weight_real, weight_imag, received)
    spectra = lax.all_to_all(beamed, "chan", split_axis=0, concat_axis=0, tiled=True)
    wide_taps = jnp.broadcast_to(filter_taps[:, :, None], (TAPS, C, FR))
    by_half = filter_taps[1:].reshape(TAPS - 1, 2, HALF)
    n1_of_lane = (lax.broadcasted_iota(jnp.int32, (FR,), 0) // 8) % 2
    packed_taps = jnp.where(n1_of_lane == 0, by_half[:, 0, :, None], by_half[:, 1, :, None])
    series, tail = synthesize(
        parity_table(0),
        parity_table(1),
        wide_taps,
        packed_taps,
        spectra.reshape(32, 8, 2, TILE, 2 * FR),
    )
    groups = lax.axis_size("tm")
    incoming = lax.ppermute(tail, "tm", [(g, g + 1) for g in range(groups - 1)])
    return patch(incoming, series)


def solution(mesh):
    placed = (
        P("chan", None, "tm"),
        P("chan", None, "tm"),
        P(None, "chan"),
        P(None, "chan"),
        P(),
        P(),
    )
    return jax.shard_map(
        per_device, mesh=mesh, in_specs=placed, out_specs=P("chan", None, "tm"), check_vma=False
    )
```

```python
import math

import jax
import jax.numpy as jnp
import ml_dtypes
import numpy as np
from jax import lax
from jax.experimental import pallas as pl
from jax.experimental.pallas import tpu as pltpu
from jax.sharding import PartitionSpec as P

C = 1024
TAPS = 4
TILE = 16
FR = 128
TWO_PI = 6.283185307179586
VMEM_MOST = 60 * 2**20


def swap_matrix():
    row = lax.broadcasted_iota(jnp.int32, (256, 256), 0)
    col = lax.broadcasted_iota(jnp.int32, (256, 256), 1)
    hit = (row // TILE == col % TILE) & (row % TILE == col // TILE)
    return jnp.where(hit, 1.0, 0.0).astype(jnp.bfloat16)


def parity_table(parity):
    sample = np.arange(C // 2)[:, None]
    channel = 2 * np.arange(C // 2)[None, :] + parity
    phases = TWO_PI / C * (sample * channel % C)
    both = np.concatenate([np.cos(phases), np.sin(phases)], axis=0) / math.sqrt(C)
    return both.astype(np.float32).astype(ml_dtypes.bfloat16)


def circle(turns):
    rest = turns - jnp.round(turns)
    half = math.pi * rest
    square = half * half
    sine = jnp.full_like(half, SIN_TERMS[-1])
    for term in SIN_TERMS[-2::-1]:
        sine = sine * square + term
    sine = sine * half
    cosine = jnp.full_like(half, COS_TERMS[-1])
    for term in COS_TERMS[-2::-1]:
        cosine = cosine * square + term
    return 1.0 - 2.0 * sine * sine, 2.0 * sine * cosine


SIN_TERMS = [(-1) ** i / math.factorial(2 * i + 1) for i in range(8)]
COS_TERMS = [(-1) ** i / math.factorial(2 * i) for i in range(8)]


SC_STEP = 128
CB = 64


def scale_kernel(exp_ref, volt_ref, out_ref, perm_ref):
    step = pl.program_id(0)

    @pl.when(step == 0)
    def _():
        perm_ref[...] = swap_matrix()

    station = lax.broadcasted_iota(jnp.int32, (TILE, 2 * FR), 0)
    for block in range(SC_STEP // CB):
        power = jnp.zeros((TILE, 2 * FR), jnp.int32)
        for s in range(TILE):
            power = jnp.where(station == s, exp_ref[s, step * (SC_STEP // CB) + block], power)
        factor = jnp.exp2(power.astype(jnp.float32)).astype(jnp.bfloat16).astype(jnp.float32)
        for part in range(CB // TILE):
            start = block * CB + part * TILE
            rows = volt_ref[:, start : start + TILE, :].reshape(256, 2 * FR)
            moved = jnp.dot(perm_ref[...], rows, preferred_element_type=jnp.float32)
            scaled = moved.reshape(TILE, TILE, 2 * FR) * factor[None]
            out_ref[start : start + TILE] = scaled.astype(jnp.bfloat16)


def scale_and_turn(voltages, exponents):
    return pl.pallas_call(
        scale_kernel,
        grid=(C // SC_STEP,),
        in_specs=[
            pl.BlockSpec(memory_space=pltpu.SMEM),
            pl.BlockSpec((TILE, SC_STEP, 2 * FR), lambda i: (0, i, 0)),
        ],
        out_specs=pl.BlockSpec((SC_STEP, TILE, 2 * FR), lambda i: (i, 0, 0)),
        out_shape=jax.ShapeDtypeStruct((C, TILE, 2 * FR), jnp.bfloat16),
        scratch_shapes=[pltpu.VMEM((256, 256), jnp.bfloat16)],
        compiler_params=pltpu.CompilerParams(vmem_limit_bytes=VMEM_MOST),
        name="scale",
    )(exponents, voltages)


CHUNK = 4
CHUNKS = 16 // CHUNK
BEAMS, STATIONS = 256, 512


def beam_kernel(
    start_ref,
    gr_ref,
    gi_ref,
    delay_ref,
    x_hbm,
    out_hbm,
    x_ref,
    out_ref,
    beams_ref,
    perm_ref,
    weight_a,
    weight_b,
    er_ref,
    ei_ref,
    sr_ref,
    si_ref,
    in_sems,
    out_sems,
):
    def arrival(q, j):
        part = pl.ds(j * CHUNK, CHUNK)
        return pltpu.make_async_copy(x_hbm.at[:, part, q], x_ref.at[q, :, part], in_sems.at[q, j])

    def departure(q):
        return pltpu.make_async_copy(out_ref.at[q], out_hbm.at[:, q], out_sems.at[q])

    for q in range(2):
        for j in range(CHUNKS):
            arrival(q, j).start()
    perm_ref[...] = swap_matrix()

    first = (start_ref[0].astype(jnp.float32) + 0.5) / C - 0.5
    for rows in range(0, BEAMS, 128):
        delay = jnp.transpose(delay_ref[:, rows : rows + 128])
        sr_ref[rows : rows + 128, :] = delay
    for rows in range(0, BEAMS, TILE):
        part = pl.ds(rows, TILE)
        delay = sr_ref[part, :]
        cosine, sine = circle(delay * first)
        er_ref[part, :] = cosine
        ei_ref[part, :] = -sine
        cosine, sine = circle(delay * (2.0 / C))
        sr_ref[part, :] = cosine
        si_ref[part, :] = -sine

    scale_factor = 1.0 / math.sqrt(STATIONS)

    def weigh(c, weight_ref):
        gr = gr_ref[pl.ds(c, 1), :] * scale_factor
        gi = gi_ref[pl.ds(c, 1), :] * scale_factor
        for rows in range(0, BEAMS, TILE):
            part = pl.ds(rows, TILE)
            er, ei = er_ref[part, :], ei_ref[part, :]
            weight_ref[part, :] = (gr * er - gi * ei).astype(jnp.bfloat16)
            weight_ref[pl.ds(BEAMS + rows, TILE), :] = (gi * er + gr * ei).astype(jnp.bfloat16)
            sr, si = sr_ref[part, :], si_ref[part, :]
            er_ref[part, :] = er * sr - ei * si
            ei_ref[part, :] = ei * sr + er * si

    def multiply(q, i, weight_ref):
        x = x_ref[q, :, i].reshape(STATIONS, 2 * FR)
        product = jnp.dot(weight_ref[...], x, preferred_element_type=jnp.float32)
        real = product[:BEAMS, :FR] - product[BEAMS:, FR:]
        imag = product[:BEAMS, FR:] + product[BEAMS:, :FR]
        beams_ref[i, :, :FR] = real.astype(jnp.bfloat16)
        beams_ref[i, :, FR:] = imag.astype(jnp.bfloat16)

    for q in range(2):
        if q == 1:
            for rows in range(0, BEAMS, 128):
                er_ref[rows : rows + 128, :] = jnp.transpose(delay_ref[:, rows : rows + 128])
            for rows in range(0, BEAMS, TILE):
                part = pl.ds(rows, TILE)
                cosine, sine = circle(er_ref[part, :] * (first + 1.0 / C))
                er_ref[part, :] = cosine
                ei_ref[part, :] = -sine

        def chunk(j, carry, q=q):
            arrival(q, j).wait()
            buffers = (weight_a, weight_b)
            for k in range(CHUNK):
                i = j * CHUNK + k
                weigh(2 * i + q, buffers[k % 2])
                multiply(q, i, buffers[k % 2])
            return carry

        lax.fori_loop(0, CHUNKS, chunk, 0)

        def turn(group, carry, q=q):
            part = pl.ds(pl.multiple_of(group * TILE, TILE), TILE)
            rows = beams_ref[:, part, :].reshape(256, 2 * FR)
            moved = jnp.dot(perm_ref[...], rows, preferred_element_type=jnp.float32)
            out_ref[q, part] = moved.reshape(TILE, TILE, 2 * FR).astype(jnp.bfloat16)
            return carry

        lax.fori_loop(0, BEAMS // TILE, turn, 0, unroll=4)
        departure(q).start()
    for q in range(2):
        departure(q).wait()


def form_beams(chan_start, gain_real, gain_imag, delays, received):
    whole = pl.BlockSpec(memory_space=pltpu.VMEM)
    remote = pl.BlockSpec(memory_space=pl.ANY)
    phasor = pltpu.VMEM((BEAMS, STATIONS), jnp.float32)
    weight = pltpu.VMEM((2 * BEAMS, STATIONS), jnp.bfloat16)
    return pl.pallas_call(
        beam_kernel,
        in_specs=[pl.BlockSpec(memory_space=pltpu.SMEM), whole, whole, whole, remote],
        out_specs=remote,
        out_shape=jax.ShapeDtypeStruct((BEAMS, 2, TILE, 2 * FR), jnp.bfloat16),
        scratch_shapes=[
            pltpu.VMEM((2, 32, 16, TILE, 2 * FR), jnp.bfloat16),
            pltpu.VMEM((2, BEAMS, TILE, 2 * FR), jnp.bfloat16),
            pltpu.VMEM((16, BEAMS, 2 * FR), jnp.bfloat16),
            pltpu.VMEM((256, 256), jnp.bfloat16),
            weight,
            weight,
            phasor,
            phasor,
            phasor,
            phasor,
            pltpu.SemaphoreType.DMA((2, CHUNKS)),
            pltpu.SemaphoreType.DMA((2,)),
        ],
        compiler_params=pltpu.CompilerParams(vmem_limit_bytes=58 * 2**20),
        name="beamform",
    )(chan_start, gain_real, gain_imag, delays, received.reshape(32, 16, 2, TILE, 2 * FR))


HALF = C // 2
ROWS = 64
LOCAL_BEAMS = 8


def transform(te_ref, to_ref, y_ref, beam, even_ref, odd_ref):
    even = y_ref[:, beam, 0].reshape(HALF, 2 * FR)
    odd = y_ref[:, beam, 1].reshape(HALF, 2 * FR)
    even_ref[...] = jnp.dot(te_ref[...], even, preferred_element_type=jnp.float32)
    odd_ref[...] = jnp.dot(to_ref[...], odd, preferred_element_type=jnp.float32)


def combine(taps_ref, beam, even_ref, odd_ref, pack_ref, out_ref):
    lane = lax.broadcasted_iota(jnp.int32, (ROWS, FR), 1)
    slot = lane // 4
    row = lax.rem(beam + LOCAL_BEAMS + 1, LOCAL_BEAMS + 1)
    for r in range(0, HALF, ROWS):
        cos_rows, sin_rows = pl.ds(r, ROWS), pl.ds(HALF + r, ROWS)
        parts = []
        for ref in (even_ref, odd_ref):
            real = ref[cos_rows, :FR] - ref[sin_rows, FR:]
            imag = ref[sin_rows, :FR] + ref[cos_rows, FR:]
            parts.append((real, imag))
        packed = pack_ref[cos_rows, :]
        for n1 in range(2):
            rows = pl.ds(n1 * HALF + r, ROWS)
            for ri in range(2):
                a, b = parts[0][ri], parts[1][ri]
                signal = a + b if n1 == 0 else a - b
                total = taps_ref[0, rows, :] * signal
                for k in range(1, TAPS):
                    shifted = jnp.where(lane >= k, pltpu.roll(signal, k, 1), 0.0)
                    total += taps_ref[k, rows, :] * shifted
                out_ref[row, rows, ri * FR : (ri + 1) * FR] = total.astype(jnp.bfloat16)
                where = beam * 4 + n1 * 2 + ri
                packed = jnp.where(
                    slot == where, pltpu.roll(signal, lax.rem(where * 4 + 4 + FR, FR), 1), packed
                )
        pack_ref[cos_rows, :] = packed


def synth_kernel(te_hbm, to_hbm, narrow_ref, y_ref, out_ref, tail_ref, *scratch):
    buffers, (pack_ref, te_ref, to_ref, taps_ref, sems) = (scratch[0:2], scratch[2:4]), scratch[4:]
    step = pl.program_id(0)
    last = pl.num_programs(0) - 1

    @pl.when(step == 0)
    def _():
        copies = [
            pltpu.make_async_copy(te_hbm, te_ref, sems.at[0]),
            pltpu.make_async_copy(to_hbm, to_ref, sems.at[1]),
        ]
        for copy in copies:
            copy.start()
        narrow = narrow_ref[...]
        columns = jnp.transpose(jnp.concatenate([narrow, narrow], axis=0))
        for k in range(TAPS):
            taps_ref[k] = jnp.broadcast_to(columns[:, k : k + 1], (C, FR))
        for copy in copies:
            copy.wait()

    def half(i):
        done = 2 * step + i - 1
        transform(te_ref, to_ref, y_ref, i, *buffers[i])
        combine(taps_ref, done, *buffers[1 - i], pack_ref, out_ref)

    half(0)

    @pl.when(step < last)
    def _():
        half(1)

    @pl.when(step == last)
    def _():
        lane = lax.broadcasted_iota(jnp.int32, (ROWS, FR), 1)
        for r in range(0, HALF, ROWS):
            rows = pl.ds(r, ROWS)
            packed = pack_ref[rows, :]
            total = jnp.zeros((ROWS, FR), jnp.float32)
            for k in range(1, TAPS):
                moved = jnp.where(lane % 4 < k, pltpu.roll(packed, FR - (4 - k), 1), 0.0)
                taps = jnp.where(
                    lane // 8 % 2 == 0, taps_ref[k, rows, :], taps_ref[k, pl.ds(HALF + r, ROWS), :]
                )
                total += taps * moved
            tail_ref[rows, :] = total.astype(jnp.bfloat16)


def synthesize(filter_taps, received):
    whole = pl.BlockSpec(memory_space=pltpu.VMEM)
    remote = pl.BlockSpec(memory_space=pl.ANY)
    steps = LOCAL_BEAMS // 2 + 1
    product = pltpu.VMEM((C, 2 * FR), jnp.float32)
    table = pltpu.VMEM((C, HALF), jnp.bfloat16)
    return pl.pallas_call(
        synth_kernel,
        grid=(steps,),
        in_specs=[
            remote,
            remote,
            whole,
            pl.BlockSpec(
                (32, 2, 2, TILE, 2 * FR), lambda g: (0, jnp.minimum(g, steps - 2), 0, 0, 0)
            ),
        ],
        out_specs=[whole, whole],
        out_shape=[
            jax.ShapeDtypeStruct((LOCAL_BEAMS + 1, C, 2 * FR), jnp.bfloat16),
            jax.ShapeDtypeStruct((HALF, FR), jnp.bfloat16),
        ],
        scratch_shapes=[product] * 4
        + [
            pltpu.VMEM((HALF, FR), jnp.float32),
            table,
            table,
            pltpu.VMEM((TAPS, C, FR), jnp.float32),
            pltpu.SemaphoreType.DMA((2,)),
        ],
        compiler_params=pltpu.CompilerParams(vmem_limit_bytes=40 * 2**20),
        name="synthesis",
    )(jnp.asarray(parity_table(0)), jnp.asarray(parity_table(1)), filter_taps, received)


def patch_kernel(in_ref, series_ref, out_ref):
    beam = pl.program_id(0)
    lane = lax.broadcasted_iota(jnp.int32, (FR, 2 * FR), 0)
    target = lax.broadcasted_iota(jnp.int32, (FR, 2 * FR), 1)
    frame, ri = target % FR, target // FR
    for n1 in range(2):
        slot = beam * 4 + n1 * 2 + ri
        spread = jnp.where((frame < TAPS - 1) & (lane == slot * 4 + frame), 1.0, 0.0)
        rows = pl.ds(n1 * HALF, HALF)
        head = jnp.dot(
            in_ref[...], spread.astype(jnp.bfloat16), preferred_element_type=jnp.float32
        )
        out_ref[0, rows, :] = (series_ref[beam, rows, :].astype(jnp.float32) + head).astype(
            jnp.bfloat16
        )


def patch(incoming, series):
    whole = pl.BlockSpec(memory_space=pltpu.VMEM)
    return pl.pallas_call(
        patch_kernel,
        grid=(LOCAL_BEAMS,),
        in_specs=[whole, whole],
        out_specs=pl.BlockSpec((1, C, 2 * FR), lambda b: (b, 0, 0)),
        out_shape=jax.ShapeDtypeStruct((LOCAL_BEAMS, C, 2 * FR), jnp.bfloat16),
        compiler_params=pltpu.CompilerParams(vmem_limit_bytes=16 * 2**20),
        name="patch",
    )(incoming, series)


def per_device(voltages, exponents, gain_real, gain_imag, delays, filter_taps):
    local_count = gain_real.shape[1]
    chan_start = (lax.axis_index("chan") * local_count).astype(jnp.int32).reshape(1)
    turned = scale_and_turn(voltages, exponents.reshape(TILE, -1))
    turned, chan_start = lax.optimization_barrier((turned, chan_start))
    received = lax.all_to_all(turned, "chan", split_axis=0, concat_axis=0, tiled=True)
    beamed = form_beams(
        chan_start, jnp.transpose(gain_real), jnp.transpose(gain_imag), delays, received
    )
    spectra = lax.all_to_all(beamed, "chan", split_axis=0, concat_axis=0, tiled=True)
    series, tail = synthesize(filter_taps, spectra.reshape(32, LOCAL_BEAMS, 2, TILE, 2 * FR))
    groups = lax.axis_size("tm")
    incoming = lax.ppermute(tail, "tm", [(g, g + 1) for g in range(groups - 1)])
    return patch(incoming, series)


def solution(mesh):
    placed = (
        P("chan", None, "tm"),
        P("chan", None, "tm"),
        P(None, "chan"),
        P(None, "chan"),
        P(),
        P(),
    )
    return jax.shard_map(
        per_device, mesh=mesh, in_specs=placed, out_specs=P("chan", None, "tm"), check_vma=False
    )
```

```python
import math

import jax
import jax.numpy as jnp
import ml_dtypes
import numpy as np
from jax import lax
from jax.experimental import pallas as pl
from jax.experimental.pallas import tpu as pltpu
from jax.sharding import PartitionSpec as P

C = 1024
TAPS = 4
TILE = 16
FR = 128
TWO_PI = 6.283185307179586
VMEM_MOST = 60 * 2**20
SYNTH_VMEM = 32 * 2**20
BEAM_VMEM = 36 * 2**20


def swap_matrix():
    row = lax.broadcasted_iota(jnp.int32, (256, 256), 0)
    col = lax.broadcasted_iota(jnp.int32, (256, 256), 1)
    hit = (row // TILE == col % TILE) & (row % TILE == col // TILE)
    return jnp.where(hit, 1.0, 0.0).astype(jnp.bfloat16)


def parity_table(parity):
    sample = np.arange(C // 2)[:, None]
    channel = 2 * np.arange(C // 2)[None, :] + parity
    phases = TWO_PI / C * (sample * channel % C)
    both = np.concatenate([np.cos(phases), np.sin(phases)], axis=0) / math.sqrt(C)
    return both.astype(np.float32).astype(ml_dtypes.bfloat16)


def circle(turns):
    rest = turns - jnp.round(turns)
    half = math.pi * rest
    square = half * half
    sine = jnp.full_like(half, SIN_TERMS[-1])
    for term in SIN_TERMS[-2::-1]:
        sine = sine * square + term
    sine = sine * half
    cosine = jnp.full_like(half, COS_TERMS[-1])
    for term in COS_TERMS[-2::-1]:
        cosine = cosine * square + term
    return 1.0 - 2.0 * sine * sine, 2.0 * sine * cosine


SIN_TERMS = [(-1) ** i / math.factorial(2 * i + 1) for i in range(7)]
COS_TERMS = [(-1) ** i / math.factorial(2 * i) for i in range(7)]


SC_STEP = 128
CB = 64


def scale_kernel(exp_ref, volt_hbm, out_hbm, volt_ref, out_ref, perm_ref, in_sems, out_sems):
    def arrival(j):
        part = pl.ds(j * SC_STEP, SC_STEP)
        return pltpu.make_async_copy(volt_hbm.at[:, part], volt_ref.at[:, part], in_sems.at[j])

    def departure(j):
        part = pl.ds(j * SC_STEP, SC_STEP)
        return pltpu.make_async_copy(out_ref.at[part], out_hbm.at[part], out_sems.at[j])

    steps = C // SC_STEP
    for j in range(steps):
        arrival(j).start()
    perm_ref[...] = swap_matrix()
    station = lax.broadcasted_iota(jnp.int32, (TILE, 2 * FR), 0)

    def scale(j, carry):
        arrival(j).wait()
        for block in range(SC_STEP // CB):
            power = jnp.zeros((TILE, 2 * FR), jnp.int32)
            for s in range(TILE):
                power = jnp.where(station == s, exp_ref[s, j * (SC_STEP // CB) + block], power)
            factor = jnp.exp2(power.astype(jnp.float32)).astype(jnp.bfloat16).astype(jnp.float32)
            for part in range(CB // TILE):
                start = pl.multiple_of(j * SC_STEP + block * CB + part * TILE, TILE)
                rows = volt_ref[:, pl.ds(start, TILE), :].reshape(256, 2 * FR)
                moved = jnp.dot(perm_ref[...], rows, preferred_element_type=jnp.float32)
                scaled = moved.reshape(TILE, TILE, 2 * FR) * factor[None]
                out_ref[pl.ds(start, TILE)] = scaled.astype(jnp.bfloat16)
        departure(j).start()
        return carry

    lax.fori_loop(0, steps, scale, 0)
    for j in range(steps):
        departure(j).wait()


def scale_and_turn(voltages, exponents):
    remote = pl.BlockSpec(memory_space=pl.ANY)
    return pl.pallas_call(
        scale_kernel,
        in_specs=[pl.BlockSpec(memory_space=pltpu.SMEM), remote],
        out_specs=remote,
        out_shape=jax.ShapeDtypeStruct((C, TILE, 2 * FR), jnp.bfloat16),
        scratch_shapes=[
            pltpu.VMEM((TILE, C, 2 * FR), jnp.bfloat16),
            pltpu.VMEM((C, TILE, 2 * FR), jnp.bfloat16),
            pltpu.VMEM((256, 256), jnp.bfloat16),
            pltpu.SemaphoreType.DMA((C // SC_STEP,)),
            pltpu.SemaphoreType.DMA((C // SC_STEP,)),
        ],
        compiler_params=pltpu.CompilerParams(vmem_limit_bytes=VMEM_MOST),
        name="scale",
    )(exponents, voltages)


CHUNK = 4
CHUNKS = 16 // CHUNK
BEAMS, STATIONS = 256, 512


def beam_kernel(
    start_ref,
    gr_ref,
    gi_ref,
    delay_ref,
    x_ref,
    out_hbm,
    out_ref,
    beams_even,
    beams_odd,
    perm_ref,
    weight_a,
    weight_b,
    er_ref,
    ei_ref,
    pr_ref,
    pi_ref,
    two_ref,
    gain_ref,
    out_sems,
):
    def departure(q):
        return pltpu.make_async_copy(out_ref.at[q], out_hbm.at[:, q], out_sems.at[q])

    beams_refs = (beams_even, beams_odd)
    perm_ref[...] = swap_matrix()

    first = (start_ref[0].astype(jnp.float32) + 0.5) / C - 0.5
    for rows in range(0, BEAMS, 128):
        two_ref[rows : rows + 128, :] = jnp.transpose(delay_ref[:, rows : rows + 128])
    for rows in range(0, BEAMS, TILE):
        part = pl.ds(rows, TILE)
        delay = two_ref[part, :]
        ar, sine = circle(delay * first)
        ai = -sine
        angle = delay * (TWO_PI / C)
        square = angle * angle
        c1 = 1.0 + square * (-1.0 / 2 + square * (1.0 / 24))
        s1 = angle * (1.0 + square * (-1.0 / 6 + square * (1.0 / 120)))
        c2, s2 = 1.0 - 2.0 * s1 * s1, 2.0 * s1 * c1
        two_ref[part, :] = 2.0 * c2
        er_ref[0, part, :], ei_ref[0, part, :] = ar, ai
        pr_ref[0, part, :], pi_ref[0, part, :] = ar * c2 - ai * s2, ai * c2 + ar * s2
        rc, rs, ic, is_ = ar * c1, ar * s1, ai * c1, ai * s1
        er_ref[1, part, :], ei_ref[1, part, :] = rc + is_, ic - rs
        pr_ref[1, part, :], pi_ref[1, part, :] = rc - is_, ic + rs

    scale_factor = 1.0 / math.sqrt(STATIONS)
    for part, ref in enumerate((gr_ref, gi_ref)):
        for c in range(ref.shape[0]):
            gain_ref[part, c] = ref[c : c + 1, :] * scale_factor

    def weigh(q, j, weight_ref, block):
        lanes = slice(block * 128, (block + 1) * 128)
        gains = []
        for k in range(CHUNK):
            c = 2 * (j * CHUNK + k) + q
            gains.append((gain_ref[0, c, :, lanes], gain_ref[1, c, :, lanes]))
        for rows in range(0, BEAMS, TILE):
            part, below = pl.ds(rows, TILE), pl.ds(BEAMS + rows, TILE)
            er, ei = er_ref[q, part, lanes], ei_ref[q, part, lanes]
            pr, pi = pr_ref[q, part, lanes], pi_ref[q, part, lanes]
            two = two_ref[part, lanes]
            for k, (gr, gi) in enumerate(gains):
                weight_ref[k, part, lanes] = (gr * er - gi * ei).astype(jnp.bfloat16)
                weight_ref[k, below, lanes] = (gi * er + gr * ei).astype(jnp.bfloat16)
                pr, er = er, two * er - pr
                pi, ei = ei, two * ei - pi
            er_ref[q, part, lanes], ei_ref[q, part, lanes] = er, ei
            pr_ref[q, part, lanes], pi_ref[q, part, lanes] = pr, pi

    def multiply(q, j, k, weight_ref):
        i = j * CHUNK + k
        x = x_ref[:, i, q].reshape(STATIONS, 2 * FR)
        product = jnp.dot(weight_ref[k], x, preferred_element_type=jnp.float32)
        real = product[:BEAMS, :FR] - product[BEAMS:, FR:]
        imag = product[:BEAMS, FR:] + product[BEAMS:, :FR]
        beams_refs[q][i, :, :FR] = real.astype(jnp.bfloat16)
        beams_refs[q][i, :, FR:] = imag.astype(jnp.bfloat16)

    def turn(q, group):
        part = pl.ds(pl.multiple_of(group * TILE, TILE), TILE)
        rows = beams_refs[q][:, part, :].reshape(256, 2 * FR)
        moved = jnp.dot(perm_ref[...], rows, preferred_element_type=jnp.float32)
        out_ref[q, part] = moved.reshape(TILE, TILE, 2 * FR).astype(jnp.bfloat16)

    groups = BEAMS // TILE
    for block in range(STATIONS // 128):
        weigh(0, 0, weight_a, block)
    for q in range(2):

        def pair(m, carry, q=q):
            for h, (now, later) in enumerate(((weight_a, weight_b), (weight_b, weight_a))):
                n = q * CHUNKS + 2 * m + h
                following = jnp.minimum(n + 1, 2 * CHUNKS - 1)
                for k in range(CHUNK):
                    multiply(q, 2 * m + h, k, now)
                    weigh(following // CHUNKS, following % CHUNKS, later, k)
                    if q == 1:
                        turn(0, 4 * (2 * m + h) + k)
            return carry

        lax.fori_loop(0, CHUNKS // 2, pair, 0)
        if q == 1:
            departure(0).start()
    for group in range(groups):
        turn(1, group)
    departure(1).start()
    for q in range(2):
        departure(q).wait()


def form_beams(chan_start, gain_real, gain_imag, delays, received):
    whole = pl.BlockSpec(memory_space=pltpu.VMEM)
    phasor = pltpu.VMEM((2, BEAMS, STATIONS), jnp.float32)
    weight = pltpu.VMEM((CHUNK, 2 * BEAMS, STATIONS), jnp.bfloat16)
    return pl.pallas_call(
        beam_kernel,
        in_specs=[pl.BlockSpec(memory_space=pltpu.SMEM), whole, whole, whole, whole],
        out_specs=pl.BlockSpec(memory_space=pl.ANY),
        out_shape=jax.ShapeDtypeStruct((BEAMS, 2, TILE, 2 * FR), jnp.bfloat16),
        scratch_shapes=[
            pltpu.VMEM((2, BEAMS, TILE, 2 * FR), jnp.bfloat16),
            pltpu.VMEM((16, BEAMS, 2 * FR), jnp.bfloat16),
            pltpu.VMEM((16, BEAMS, 2 * FR), jnp.bfloat16),
            pltpu.VMEM((256, 256), jnp.bfloat16),
            weight,
            weight,
            phasor,
            phasor,
            phasor,
            phasor,
            pltpu.VMEM((BEAMS, STATIONS), jnp.float32),
            pltpu.VMEM((2, gain_real.shape[0], 1, STATIONS), jnp.float32),
            pltpu.SemaphoreType.DMA((2,)),
        ],
        compiler_params=pltpu.CompilerParams(vmem_limit_bytes=BEAM_VMEM),
        name="beamform",
    )(chan_start, gain_real, gain_imag, delays, received.reshape(32, 16, 2, TILE, 2 * FR))


HALF = C // 2
ROWS = 64
LOCAL_BEAMS = 8


def transform(te_ref, to_ref, y_ref, beam, even_ref, odd_ref):
    even = y_ref[:, beam, 0].reshape(HALF, 2 * FR)
    odd = y_ref[:, beam, 1].reshape(HALF, 2 * FR)
    even_ref[...] = jnp.dot(te_ref[...], even, preferred_element_type=jnp.float32)
    odd_ref[...] = jnp.dot(to_ref[...], odd, preferred_element_type=jnp.float32)


def combine(taps_ref, beam, even_ref, odd_ref, pack_ref, out_ref):
    lane = lax.broadcasted_iota(jnp.int32, (ROWS, FR), 1)
    slot = lane // 4
    row = lax.rem(beam + LOCAL_BEAMS + 1, LOCAL_BEAMS + 1)
    for r in range(0, HALF, ROWS):
        cos_rows, sin_rows = pl.ds(r, ROWS), pl.ds(HALF + r, ROWS)
        parts = []
        for ref in (even_ref, odd_ref):
            real = ref[cos_rows, :FR] - ref[sin_rows, FR:]
            imag = ref[sin_rows, :FR] + ref[cos_rows, FR:]
            parts.append((real, imag))
        packed = pack_ref[cos_rows, :]
        for n1 in range(2):
            rows = pl.ds(n1 * HALF + r, ROWS)
            for ri in range(2):
                a, b = parts[0][ri], parts[1][ri]
                signal = a + b if n1 == 0 else a - b
                total = taps_ref[0, rows, :] * signal
                for k in range(1, TAPS):
                    shifted = jnp.where(lane >= k, pltpu.roll(signal, k, 1), 0.0)
                    total += taps_ref[k, rows, :] * shifted
                out_ref[row, rows, ri * FR : (ri + 1) * FR] = total.astype(jnp.bfloat16)
                where = beam * 4 + n1 * 2 + ri
                packed = jnp.where(
                    slot == where, pltpu.roll(signal, lax.rem(where * 4 + 4 + FR, FR), 1), packed
                )
        pack_ref[cos_rows, :] = packed


def synth_kernel(te_ref, to_ref, narrow_ref, y_ref, out_ref, tail_ref, *scratch):
    buffers, (pack_ref, taps_ref) = (scratch[0:2], scratch[2:4]), scratch[4:]
    step = pl.program_id(0)

    @pl.when(step == 0)
    def _():
        narrow = narrow_ref[...]
        columns = jnp.transpose(jnp.concatenate([narrow, narrow], axis=0))
        for k in range(TAPS):
            taps_ref[k] = jnp.broadcast_to(columns[:, k : k + 1], (C, FR))

    last = pl.num_programs(0) - 1

    def half(i):
        done = 2 * step + i - 1
        arriving = jnp.minimum(2 * step + i, LOCAL_BEAMS - 1)
        transform(te_ref, to_ref, y_ref, arriving, *buffers[i])
        combine(taps_ref, done, *buffers[1 - i], pack_ref, out_ref)

    half(0)

    @pl.when(step < last)
    def _():
        half(1)

    @pl.when(step == last)
    def _():
        lane = lax.broadcasted_iota(jnp.int32, (ROWS, FR), 1)
        for r in range(0, HALF, ROWS):
            rows = pl.ds(r, ROWS)
            packed = pack_ref[rows, :]
            total = jnp.zeros((ROWS, FR), jnp.float32)
            for k in range(1, TAPS):
                moved = jnp.where(lane % 4 < k, pltpu.roll(packed, FR - (4 - k), 1), 0.0)
                taps = jnp.where(
                    lane // 8 % 2 == 0, taps_ref[k, rows, :], taps_ref[k, pl.ds(HALF + r, ROWS), :]
                )
                total += taps * moved
            tail_ref[rows, :] = total.astype(jnp.bfloat16)


def synthesize(filter_taps, received):
    whole = pl.BlockSpec(memory_space=pltpu.VMEM)
    steps = LOCAL_BEAMS // 2 + 1
    product = pltpu.VMEM((C, 2 * FR), jnp.float32)
    return pl.pallas_call(
        synth_kernel,
        grid=(steps,),
        in_specs=[whole] * 4,
        out_specs=[whole, whole],
        out_shape=[
            jax.ShapeDtypeStruct((LOCAL_BEAMS + 1, C, 2 * FR), jnp.bfloat16),
            jax.ShapeDtypeStruct((HALF, FR), jnp.bfloat16),
        ],
        scratch_shapes=[product] * 4
        + [pltpu.VMEM((HALF, FR), jnp.float32), pltpu.VMEM((TAPS, C, FR), jnp.float32)],
        compiler_params=pltpu.CompilerParams(vmem_limit_bytes=SYNTH_VMEM),
        name="synthesis",
    )(jnp.asarray(parity_table(0)), jnp.asarray(parity_table(1)), filter_taps, received)


PATCH_BEAMS = 4


def patch_kernel(in_ref, series_ref, out_ref):
    lane = lax.broadcasted_iota(jnp.int32, (FR, 2 * FR), 0)
    target = lax.broadcasted_iota(jnp.int32, (FR, 2 * FR), 1)
    frame, ri = target % FR, target // FR
    for i in range(PATCH_BEAMS):
        beam = pl.program_id(0) * PATCH_BEAMS + i
        for n1 in range(2):
            slot = beam * 4 + n1 * 2 + ri
            spread = jnp.where((frame < TAPS - 1) & (lane == slot * 4 + frame), 1.0, 0.0)
            rows = pl.ds(n1 * HALF, HALF)
            head = jnp.dot(
                in_ref[...], spread.astype(jnp.bfloat16), preferred_element_type=jnp.float32
            )
            out_ref[i, rows, :] = (series_ref[beam, rows, :].astype(jnp.float32) + head).astype(
                jnp.bfloat16
            )


def patch(incoming, series):
    whole = pl.BlockSpec(memory_space=pltpu.VMEM)
    return pl.pallas_call(
        patch_kernel,
        grid=(LOCAL_BEAMS // PATCH_BEAMS,),
        in_specs=[whole, whole],
        out_specs=pl.BlockSpec((PATCH_BEAMS, C, 2 * FR), lambda b: (b, 0, 0)),
        out_shape=jax.ShapeDtypeStruct((LOCAL_BEAMS, C, 2 * FR), jnp.bfloat16),
        compiler_params=pltpu.CompilerParams(vmem_limit_bytes=16 * 2**20),
        name="patch",
    )(incoming, series)


def per_device(voltages, exponents, gain_real, gain_imag, delays, filter_taps):
    local_count = gain_real.shape[1]
    chan_start = (lax.axis_index("chan") * local_count).astype(jnp.int32).reshape(1)
    turned = scale_and_turn(voltages, exponents.reshape(TILE, -1))
    turned, chan_start = lax.optimization_barrier((turned, chan_start))
    received = lax.all_to_all(turned, "chan", split_axis=0, concat_axis=0, tiled=True)
    beamed = form_beams(
        chan_start, jnp.transpose(gain_real), jnp.transpose(gain_imag), delays, received
    )
    spectra = lax.all_to_all(beamed, "chan", split_axis=0, concat_axis=0, tiled=True)
    series, tail = synthesize(filter_taps, spectra.reshape(32, LOCAL_BEAMS, 2, TILE, 2 * FR))
    groups = lax.axis_size("tm")
    incoming = lax.ppermute(tail, "tm", [(g, g + 1) for g in range(groups - 1)])
    return patch(incoming, series)


def solution(mesh):
    placed = (
        P("chan", None, "tm"),
        P("chan", None, "tm"),
        P(None, "chan"),
        P(None, "chan"),
        P(),
        P(),
    )
    return jax.shard_map(
        per_device, mesh=mesh, in_specs=placed, out_specs=P("chan", None, "tm"), check_vma=False
    )
```

```python
import math

import jax
import jax.numpy as jnp
import ml_dtypes
import numpy as np
from jax import lax
from jax.experimental import pallas as pl
from jax.experimental.pallas import tpu as pltpu
from jax.sharding import PartitionSpec as P

C = 1024
TAPS = 4
TILE = 16
FR = 128
TWO_PI = 6.283185307179586
VMEM_MOST = 60 * 2**20
SYNTH_VMEM = 32 * 2**20
BEAM_VMEM = 36 * 2**20


def swap_matrix():
    row = lax.broadcasted_iota(jnp.int32, (256, 256), 0)
    col = lax.broadcasted_iota(jnp.int32, (256, 256), 1)
    hit = (row // TILE == col % TILE) & (row % TILE == col // TILE)
    return jnp.where(hit, 1.0, 0.0).astype(jnp.bfloat16)


def parity_table(parity):
    sample = np.arange(C // 2)[:, None]
    channel = 2 * np.arange(C // 2)[None, :] + parity
    phases = TWO_PI / C * (sample * channel % C)
    both = np.concatenate([np.cos(phases), np.sin(phases)], axis=0) / math.sqrt(C)
    return both.astype(np.float32).astype(ml_dtypes.bfloat16)


def circle(turns):
    rest = turns - jnp.round(turns)
    half = math.pi * rest
    square = half * half
    sine = jnp.full_like(half, SIN_TERMS[-1])
    for term in SIN_TERMS[-2::-1]:
        sine = sine * square + term
    sine = sine * half
    cosine = jnp.full_like(half, COS_TERMS[-1])
    for term in COS_TERMS[-2::-1]:
        cosine = cosine * square + term
    return 1.0 - 2.0 * sine * sine, 2.0 * sine * cosine


SIN_TERMS = [(-1) ** i / math.factorial(2 * i + 1) for i in range(7)]
COS_TERMS = [(-1) ** i / math.factorial(2 * i) for i in range(7)]


SC_STEP = 128
CB = 64


def scale_kernel(exp_ref, volt_hbm, out_hbm, volt_ref, out_ref, perm_ref, in_sems, out_sems):
    def arrival(j):
        part = pl.ds(j * SC_STEP, SC_STEP)
        return pltpu.make_async_copy(volt_hbm.at[:, part], volt_ref.at[:, part], in_sems.at[j])

    def departure(j):
        part = pl.ds(j * SC_STEP, SC_STEP)
        return pltpu.make_async_copy(out_ref.at[part], out_hbm.at[part], out_sems.at[j])

    steps = C // SC_STEP
    for j in range(steps):
        arrival(j).start()
    perm_ref[...] = swap_matrix()
    station = lax.broadcasted_iota(jnp.int32, (TILE, 2 * FR), 0)

    def scale(j, carry):
        arrival(j).wait()
        for block in range(SC_STEP // CB):
            power = jnp.zeros((TILE, 2 * FR), jnp.int32)
            for s in range(TILE):
                power = jnp.where(station == s, exp_ref[s, j * (SC_STEP // CB) + block], power)
            factor = jnp.exp2(power.astype(jnp.float32)).astype(jnp.bfloat16).astype(jnp.float32)
            for part in range(CB // TILE):
                start = pl.multiple_of(j * SC_STEP + block * CB + part * TILE, TILE)
                rows = volt_ref[:, pl.ds(start, TILE), :].reshape(256, 2 * FR)
                moved = jnp.dot(perm_ref[...], rows, preferred_element_type=jnp.float32)
                scaled = moved.reshape(TILE, TILE, 2 * FR) * factor[None]
                out_ref[pl.ds(start, TILE)] = scaled.astype(jnp.bfloat16)
        departure(j).start()
        return carry

    lax.fori_loop(0, steps, scale, 0)
    for j in range(steps):
        departure(j).wait()


def scale_and_turn(voltages, exponents):
    remote = pl.BlockSpec(memory_space=pl.ANY)
    return pl.pallas_call(
        scale_kernel,
        in_specs=[pl.BlockSpec(memory_space=pltpu.SMEM), remote],
        out_specs=remote,
        out_shape=jax.ShapeDtypeStruct((C, TILE, 2 * FR), jnp.bfloat16),
        scratch_shapes=[
            pltpu.VMEM((TILE, C, 2 * FR), jnp.bfloat16),
            pltpu.VMEM((C, TILE, 2 * FR), jnp.bfloat16),
            pltpu.VMEM((256, 256), jnp.bfloat16),
            pltpu.SemaphoreType.DMA((C // SC_STEP,)),
            pltpu.SemaphoreType.DMA((C // SC_STEP,)),
        ],
        compiler_params=pltpu.CompilerParams(vmem_limit_bytes=VMEM_MOST),
        name="scale",
    )(exponents, voltages)


CHUNK = 4
CHUNKS = 16 // CHUNK
BEAMS, STATIONS = 256, 512


def beam_kernel(
    start_ref,
    gr_ref,
    gi_ref,
    delay_ref,
    x_ref,
    out_hbm,
    out_ref,
    beams_even,
    beams_odd,
    perm_ref,
    weight_a,
    weight_b,
    er_ref,
    ei_ref,
    pr_ref,
    pi_ref,
    two_ref,
    gain_ref,
    out_sems,
):
    def departure(q):
        return pltpu.make_async_copy(out_ref.at[q], out_hbm.at[:, q], out_sems.at[q])

    beams_refs = (beams_even, beams_odd)
    perm_ref[...] = swap_matrix()

    first = (start_ref[0].astype(jnp.float32) + 0.5) / C - 0.5
    for rows in range(0, BEAMS, 128):
        two_ref[rows : rows + 128, :] = jnp.transpose(delay_ref[:, rows : rows + 128])
    for rows in range(0, BEAMS, TILE):
        part = pl.ds(rows, TILE)
        delay = two_ref[part, :]
        ar, sine = circle(delay * first)
        ai = -sine
        angle = delay * (TWO_PI / C)
        square = angle * angle
        c1 = 1.0 + square * (-1.0 / 2 + square * (1.0 / 24))
        s1 = angle * (1.0 + square * (-1.0 / 6 + square * (1.0 / 120)))
        c2, s2 = 1.0 - 2.0 * s1 * s1, 2.0 * s1 * c1
        two_ref[part, :] = 2.0 * c2
        er_ref[0, part, :], ei_ref[0, part, :] = ar, ai
        pr_ref[0, part, :], pi_ref[0, part, :] = ar * c2 - ai * s2, ai * c2 + ar * s2
        rc, rs, ic, is_ = ar * c1, ar * s1, ai * c1, ai * s1
        er_ref[1, part, :], ei_ref[1, part, :] = rc + is_, ic - rs
        pr_ref[1, part, :], pi_ref[1, part, :] = rc - is_, ic + rs

    scale_factor = 1.0 / math.sqrt(STATIONS)
    for part, ref in enumerate((gr_ref, gi_ref)):
        for c in range(ref.shape[0]):
            gain_ref[part, c] = ref[c : c + 1, :] * scale_factor

    def weigh(q, j, weight_ref, block):
        lanes = slice(block * 128, (block + 1) * 128)
        gains = []
        for k in range(CHUNK):
            c = 2 * (j * CHUNK + k) + q
            gains.append((gain_ref[0, c, :, lanes], gain_ref[1, c, :, lanes]))
        for rows in range(0, BEAMS, TILE):
            part, below = pl.ds(rows, TILE), pl.ds(BEAMS + rows, TILE)
            er, ei = er_ref[q, part, lanes], ei_ref[q, part, lanes]
            pr, pi = pr_ref[q, part, lanes], pi_ref[q, part, lanes]
            two = two_ref[part, lanes]
            for k, (gr, gi) in enumerate(gains):
                weight_ref[k, part, lanes] = (gr * er - gi * ei).astype(jnp.bfloat16)
                weight_ref[k, below, lanes] = (gi * er + gr * ei).astype(jnp.bfloat16)
                pr, er = er, two * er - pr
                pi, ei = ei, two * ei - pi
            er_ref[q, part, lanes], ei_ref[q, part, lanes] = er, ei
            pr_ref[q, part, lanes], pi_ref[q, part, lanes] = pr, pi

    def multiply(q, j, k, weight_ref):
        i = j * CHUNK + k
        x = x_ref[:, i, q].reshape(STATIONS, 2 * FR)
        product = jnp.dot(weight_ref[k], x, preferred_element_type=jnp.float32)
        real = product[:BEAMS, :FR] - product[BEAMS:, FR:]
        imag = product[:BEAMS, FR:] + product[BEAMS:, :FR]
        beams_refs[q][i, :, :FR] = real.astype(jnp.bfloat16)
        beams_refs[q][i, :, FR:] = imag.astype(jnp.bfloat16)

    def turn(q, group):
        part = pl.ds(pl.multiple_of(group * TILE, TILE), TILE)
        rows = beams_refs[q][:, part, :].reshape(256, 2 * FR)
        moved = jnp.dot(perm_ref[...], rows, preferred_element_type=jnp.float32)
        out_ref[q, part] = moved.reshape(TILE, TILE, 2 * FR).astype(jnp.bfloat16)

    groups = BEAMS // TILE
    for block in range(STATIONS // 128):
        weigh(0, 0, weight_a, block)
    for q in range(2):

        def pair(m, carry, q=q):
            for h, (now, later) in enumerate(((weight_a, weight_b), (weight_b, weight_a))):
                n = q * CHUNKS + 2 * m + h
                following = jnp.minimum(n + 1, 2 * CHUNKS - 1)
                for k in range(CHUNK):
                    multiply(q, 2 * m + h, k, now)
                    weigh(following // CHUNKS, following % CHUNKS, later, k)
                    if q == 1:
                        turn(0, 4 * (2 * m + h) + k)
            return carry

        lax.fori_loop(0, CHUNKS // 2, pair, 0)
        if q == 1:
            departure(0).start()
    for group in range(groups):
        turn(1, group)
    departure(1).start()
    for q in range(2):
        departure(q).wait()


def form_beams(chan_start, gain_real, gain_imag, delays, received):
    whole = pl.BlockSpec(memory_space=pltpu.VMEM)
    phasor = pltpu.VMEM((2, BEAMS, STATIONS), jnp.float32)
    weight = pltpu.VMEM((CHUNK, 2 * BEAMS, STATIONS), jnp.bfloat16)
    return pl.pallas_call(
        beam_kernel,
        in_specs=[pl.BlockSpec(memory_space=pltpu.SMEM), whole, whole, whole, whole],
        out_specs=pl.BlockSpec(memory_space=pl.ANY),
        out_shape=jax.ShapeDtypeStruct((BEAMS, 2, TILE, 2 * FR), jnp.bfloat16),
        scratch_shapes=[
            pltpu.VMEM((2, BEAMS, TILE, 2 * FR), jnp.bfloat16),
            pltpu.VMEM((16, BEAMS, 2 * FR), jnp.bfloat16),
            pltpu.VMEM((16, BEAMS, 2 * FR), jnp.bfloat16),
            pltpu.VMEM((256, 256), jnp.bfloat16),
            weight,
            weight,
            phasor,
            phasor,
            phasor,
            phasor,
            pltpu.VMEM((BEAMS, STATIONS), jnp.float32),
            pltpu.VMEM((2, gain_real.shape[0], 1, STATIONS), jnp.float32),
            pltpu.SemaphoreType.DMA((2,)),
        ],
        compiler_params=pltpu.CompilerParams(vmem_limit_bytes=BEAM_VMEM),
        name="beamform",
    )(chan_start, gain_real, gain_imag, delays, received.reshape(32, 16, 2, TILE, 2 * FR))


HALF = C // 2
ROWS = 64
LOCAL_BEAMS = 8


def transform(te_ref, to_ref, y_ref, beam, even_ref, odd_ref):
    even = y_ref[:, beam, 0].reshape(HALF, 2 * FR)
    odd = y_ref[:, beam, 1].reshape(HALF, 2 * FR)
    even_ref[...] = jnp.dot(te_ref[...], even, preferred_element_type=jnp.float32)
    odd_ref[...] = jnp.dot(to_ref[...], odd, preferred_element_type=jnp.float32)


def combine(taps_ref, beam, even_ref, odd_ref, pack_ref, signal_ref, out_ref):
    lane = lax.broadcasted_iota(jnp.int32, (ROWS, FR), 1)
    for r in range(0, HALF, ROWS):
        cos_rows, sin_rows = pl.ds(r, ROWS), pl.ds(HALF + r, ROWS)
        parts = []
        for ref in (even_ref, odd_ref):
            real = ref[cos_rows, :FR] - ref[sin_rows, FR:]
            imag = ref[sin_rows, :FR] + ref[cos_rows, FR:]
            parts.append((real, imag))
        for n1 in range(2):
            rows = pl.ds(n1 * HALF + r, ROWS)
            for ri in range(2):
                a, b = parts[0][ri], parts[1][ri]
                signal = a + b if n1 == 0 else a - b
                total = taps_ref[0, rows, :] * signal
                for k in range(1, TAPS):
                    shifted = jnp.where(lane >= k, pltpu.roll(signal, k, 1), 0.0)
                    total += taps_ref[k, rows, :] * shifted
                out_ref[beam, rows, ri * FR : (ri + 1) * FR] = total.astype(jnp.bfloat16)
                signal_ref[n1, cos_rows, ri * FR : (ri + 1) * FR] = signal.astype(jnp.bfloat16)
    source = lax.broadcasted_iota(jnp.int32, (2 * FR, FR), 0)
    target = lax.broadcasted_iota(jnp.int32, (2 * FR, FR), 1)
    frame, ri = source % FR - (FR - 4), source // FR
    for n1 in range(2):
        chosen = (frame >= 0) & (target == (beam * 4 + n1 * 2 + ri) * 4 + frame)
        pack_ref[...] += jnp.dot(
            signal_ref[n1],
            jnp.where(chosen, 1.0, 0.0).astype(jnp.bfloat16),
            preferred_element_type=jnp.float32,
        )


def synth_kernel(te_ref, to_ref, narrow_ref, y_ref, out_ref, tail_ref, *scratch):
    buffers, (pack_ref, taps_ref, signal_ref) = (scratch[0:2], scratch[2:4]), scratch[4:]
    step = pl.program_id(0)

    @pl.when(step == 0)
    def _():
        pack_ref[...] = jnp.zeros_like(pack_ref)
        narrow = narrow_ref[...]
        columns = jnp.transpose(jnp.concatenate([narrow, narrow], axis=0))
        for k in range(TAPS):
            taps_ref[k] = jnp.broadcast_to(columns[:, k : k + 1], (C, FR))

    last = pl.num_programs(0) - 1

    def half(i, back=True):
        transform(te_ref, to_ref, y_ref, 2 * step + i, *buffers[i])
        if back:
            combine(taps_ref, 2 * step + i - 1, *buffers[1 - i], pack_ref, signal_ref, out_ref)

    @pl.when(step == 0)
    def _():
        half(0, back=False)

    @pl.when((step > 0) & (step < last))
    def _():
        half(0)

    @pl.when(step < last)
    def _():
        half(1)

    @pl.when(step == last)
    def _():
        combine(taps_ref, LOCAL_BEAMS - 1, *buffers[1], pack_ref, signal_ref, out_ref)

    @pl.when(step == last)
    def _():
        lane = lax.broadcasted_iota(jnp.int32, (ROWS, FR), 1)
        for r in range(0, HALF, ROWS):
            rows = pl.ds(r, ROWS)
            packed = pack_ref[rows, :]
            total = jnp.zeros((ROWS, FR), jnp.float32)
            for k in range(1, TAPS):
                moved = jnp.where(lane % 4 < k, pltpu.roll(packed, FR - (4 - k), 1), 0.0)
                taps = jnp.where(
                    lane // 8 % 2 == 0, taps_ref[k, rows, :], taps_ref[k, pl.ds(HALF + r, ROWS), :]
                )
                total += taps * moved
            tail_ref[rows, :] = total.astype(jnp.bfloat16)


def synthesize(filter_taps, received):
    whole = pl.BlockSpec(memory_space=pltpu.VMEM)
    steps = LOCAL_BEAMS // 2 + 1
    product = pltpu.VMEM((C, 2 * FR), jnp.float32)
    return pl.pallas_call(
        synth_kernel,
        grid=(steps,),
        in_specs=[whole] * 4,
        out_specs=[whole, whole],
        out_shape=[
            jax.ShapeDtypeStruct((LOCAL_BEAMS, C, 2 * FR), jnp.bfloat16),
            jax.ShapeDtypeStruct((HALF, FR), jnp.bfloat16),
        ],
        scratch_shapes=[product] * 4
        + [
            pltpu.VMEM((HALF, FR), jnp.float32),
            pltpu.VMEM((TAPS, C, FR), jnp.float32),
            pltpu.VMEM((2, HALF, 2 * FR), jnp.bfloat16),
        ],
        compiler_params=pltpu.CompilerParams(vmem_limit_bytes=SYNTH_VMEM),
        name="synthesis",
    )(jnp.asarray(parity_table(0)), jnp.asarray(parity_table(1)), filter_taps, received)


PATCH_BEAMS = 4


def patch_kernel(in_ref, series_ref, out_ref):
    lane = lax.broadcasted_iota(jnp.int32, (FR, 2 * FR), 0)
    target = lax.broadcasted_iota(jnp.int32, (FR, 2 * FR), 1)
    frame, ri = target % FR, target // FR
    for i in range(PATCH_BEAMS):
        beam = pl.program_id(0) * PATCH_BEAMS + i
        for n1 in range(2):
            slot = beam * 4 + n1 * 2 + ri
            spread = jnp.where((frame < TAPS - 1) & (lane == slot * 4 + frame), 1.0, 0.0)
            rows = pl.ds(n1 * HALF, HALF)
            head = jnp.dot(
                in_ref[...], spread.astype(jnp.bfloat16), preferred_element_type=jnp.float32
            )
            out_ref[i, rows, :] = (series_ref[beam, rows, :].astype(jnp.float32) + head).astype(
                jnp.bfloat16
            )


def patch(incoming, series):
    whole = pl.BlockSpec(memory_space=pltpu.VMEM)
    return pl.pallas_call(
        patch_kernel,
        grid=(LOCAL_BEAMS // PATCH_BEAMS,),
        in_specs=[whole, whole],
        out_specs=pl.BlockSpec((PATCH_BEAMS, C, 2 * FR), lambda b: (b, 0, 0)),
        out_shape=jax.ShapeDtypeStruct((LOCAL_BEAMS, C, 2 * FR), jnp.bfloat16),
        compiler_params=pltpu.CompilerParams(vmem_limit_bytes=16 * 2**20),
        name="patch",
    )(incoming, series)


def per_device(voltages, exponents, gain_real, gain_imag, delays, filter_taps):
    local_count = gain_real.shape[1]
    chan_start = (lax.axis_index("chan") * local_count).astype(jnp.int32).reshape(1)
    turned = scale_and_turn(voltages, exponents.reshape(TILE, -1))
    turned, chan_start = lax.optimization_barrier((turned, chan_start))
    received = lax.all_to_all(turned, "chan", split_axis=0, concat_axis=0, tiled=True)
    beamed = form_beams(
        chan_start, jnp.transpose(gain_real), jnp.transpose(gain_imag), delays, received
    )
    spectra = lax.all_to_all(beamed, "chan", split_axis=0, concat_axis=0, tiled=True)
    series, tail = synthesize(filter_taps, spectra.reshape(32, LOCAL_BEAMS, 2, TILE, 2 * FR))
    groups = lax.axis_size("tm")
    incoming = lax.ppermute(tail, "tm", [(g, g + 1) for g in range(groups - 1)])
    return patch(incoming, series)


def solution(mesh):
    placed = (
        P("chan", None, "tm"),
        P("chan", None, "tm"),
        P(None, "chan"),
        P(None, "chan"),
        P(),
        P(),
    )
    return jax.shard_map(
        per_device, mesh=mesh, in_specs=placed, out_specs=P("chan", None, "tm"), check_vma=False
    )
```

```python
import math

import jax
import jax.numpy as jnp
import ml_dtypes
import numpy as np
from jax import lax
from jax.experimental import pallas as pl
from jax.experimental.pallas import tpu as pltpu
from jax.sharding import PartitionSpec as P

C = 1024
TAPS = 4
TILE = 16
FR = 128
TWO_PI = 6.283185307179586
SCALE_VMEM = 44 * 2**20
SYNTH_VMEM = 32 * 2**20
BEAM_VMEM = 36 * 2**20


def swap_matrix():
    row = lax.broadcasted_iota(jnp.int32, (256, 256), 0)
    col = lax.broadcasted_iota(jnp.int32, (256, 256), 1)
    hit = (row // TILE == col % TILE) & (row % TILE == col // TILE)
    return jnp.where(hit, 1.0, 0.0).astype(jnp.bfloat16)


def parity_table(parity):
    sample = np.arange(C // 2)[:, None]
    channel = 2 * np.arange(C // 2)[None, :] + parity
    phases = TWO_PI / C * (sample * channel % C)
    both = np.concatenate([np.cos(phases), np.sin(phases)], axis=0) / math.sqrt(C)
    return both.astype(np.float32).astype(ml_dtypes.bfloat16)


def circle(turns):
    rest = turns - jnp.round(turns)
    half = math.pi * rest
    square = half * half
    sine = jnp.full_like(half, SIN_TERMS[-1])
    for term in SIN_TERMS[-2::-1]:
        sine = sine * square + term
    sine = sine * half
    cosine = jnp.full_like(half, COS_TERMS[-1])
    for term in COS_TERMS[-2::-1]:
        cosine = cosine * square + term
    return 1.0 - 2.0 * sine * sine, 2.0 * sine * cosine


SIN_TERMS = [(-1) ** i / math.factorial(2 * i + 1) for i in range(7)]
COS_TERMS = [(-1) ** i / math.factorial(2 * i) for i in range(7)]


SC_STEP = 128
CB = 64


def scale_kernel(exp_ref, volt_hbm, out_ref, volt_ref, perm_ref, in_sems):
    def arrival(j):
        part = pl.ds(j * SC_STEP, SC_STEP)
        return pltpu.make_async_copy(volt_hbm.at[:, part], volt_ref.at[:, part], in_sems.at[j])

    steps = C // SC_STEP
    for j in range(steps):
        arrival(j).start()
    perm_ref[...] = swap_matrix()
    station = lax.broadcasted_iota(jnp.int32, (TILE, 2 * FR), 0)

    def scale(j, carry):
        arrival(j).wait()
        for block in range(SC_STEP // CB):
            power = jnp.zeros((TILE, 2 * FR), jnp.int32)
            for s in range(TILE):
                power = jnp.where(station == s, exp_ref[s, j * (SC_STEP // CB) + block], power)
            factor = jnp.exp2(power.astype(jnp.float32)).astype(jnp.bfloat16).astype(jnp.float32)
            for part in range(CB // TILE):
                start = pl.multiple_of(j * SC_STEP + block * CB + part * TILE, TILE)
                rows = volt_ref[:, pl.ds(start, TILE), :].reshape(256, 2 * FR)
                moved = jnp.dot(perm_ref[...], rows, preferred_element_type=jnp.float32)
                scaled = moved.reshape(TILE, TILE, 2 * FR) * factor[None]
                out_ref[pl.ds(start, TILE)] = scaled.astype(jnp.bfloat16)
        return carry

    lax.fori_loop(0, steps, scale, 0)


def scale_and_turn(voltages, exponents):
    remote = pl.BlockSpec(memory_space=pl.ANY)
    return pl.pallas_call(
        scale_kernel,
        in_specs=[pl.BlockSpec(memory_space=pltpu.SMEM), remote],
        out_specs=pl.BlockSpec(memory_space=pltpu.VMEM),
        out_shape=jax.ShapeDtypeStruct((C, TILE, 2 * FR), jnp.bfloat16),
        scratch_shapes=[
            pltpu.VMEM((TILE, C, 2 * FR), jnp.bfloat16),
            pltpu.VMEM((256, 256), jnp.bfloat16),
            pltpu.SemaphoreType.DMA((C // SC_STEP,)),
        ],
        compiler_params=pltpu.CompilerParams(vmem_limit_bytes=SCALE_VMEM),
        name="scale",
    )(exponents, voltages)


CHUNK = 4
CHUNKS = 16 // CHUNK
BEAMS, STATIONS = 256, 512


def beam_kernel(
    start_ref,
    gr_ref,
    gi_ref,
    delay_ref,
    x_ref,
    out_ref,
    beams_even,
    beams_odd,
    perm_ref,
    weight_a,
    weight_b,
    er_ref,
    ei_ref,
    pr_ref,
    pi_ref,
    two_ref,
    gain_ref,
):
    beams_refs = (beams_even, beams_odd)
    perm_ref[...] = swap_matrix()

    first = (start_ref[0].astype(jnp.float32) + 0.5) / C - 0.5
    for rows in range(0, BEAMS, 128):
        two_ref[rows : rows + 128, :] = jnp.transpose(delay_ref[:, rows : rows + 128])
    for rows in range(0, BEAMS, TILE):
        part = pl.ds(rows, TILE)
        delay = two_ref[part, :]
        ar, sine = circle(delay * first)
        ai = -sine
        angle = delay * (TWO_PI / C)
        square = angle * angle
        c1 = 1.0 + square * (-1.0 / 2 + square * (1.0 / 24))
        s1 = angle * (1.0 + square * (-1.0 / 6 + square * (1.0 / 120)))
        c2, s2 = 1.0 - 2.0 * s1 * s1, 2.0 * s1 * c1
        two_ref[part, :] = 2.0 * c2
        er_ref[0, part, :], ei_ref[0, part, :] = ar, ai
        pr_ref[0, part, :], pi_ref[0, part, :] = ar * c2 - ai * s2, ai * c2 + ar * s2
        rc, rs, ic, is_ = ar * c1, ar * s1, ai * c1, ai * s1
        er_ref[1, part, :], ei_ref[1, part, :] = rc + is_, ic - rs
        pr_ref[1, part, :], pi_ref[1, part, :] = rc - is_, ic + rs

    scale_factor = 1.0 / math.sqrt(STATIONS)
    for part, ref in enumerate((gr_ref, gi_ref)):
        for c in range(ref.shape[0]):
            gain_ref[part, c] = ref[c : c + 1, :] * scale_factor

    def weigh(q, j, weight_ref, block):
        lanes = slice(block * 128, (block + 1) * 128)
        gains = []
        for k in range(CHUNK):
            c = 2 * (j * CHUNK + k) + q
            gains.append((gain_ref[0, c, :, lanes], gain_ref[1, c, :, lanes]))
        for rows in range(0, BEAMS, TILE):
            part, below = pl.ds(rows, TILE), pl.ds(BEAMS + rows, TILE)
            er, ei = er_ref[q, part, lanes], ei_ref[q, part, lanes]
            pr, pi = pr_ref[q, part, lanes], pi_ref[q, part, lanes]
            two = two_ref[part, lanes]
            for k, (gr, gi) in enumerate(gains):
                weight_ref[k, part, lanes] = (gr * er - gi * ei).astype(jnp.bfloat16)
                weight_ref[k, below, lanes] = (gi * er + gr * ei).astype(jnp.bfloat16)
                pr, er = er, two * er - pr
                pi, ei = ei, two * ei - pi
            er_ref[q, part, lanes], ei_ref[q, part, lanes] = er, ei
            pr_ref[q, part, lanes], pi_ref[q, part, lanes] = pr, pi

    def multiply(q, j, k, weight_ref):
        i = j * CHUNK + k
        x = x_ref[:, i, q].reshape(STATIONS, 2 * FR)
        product = jnp.dot(weight_ref[k], x, preferred_element_type=jnp.float32)
        real = product[:BEAMS, :FR] - product[BEAMS:, FR:]
        imag = product[:BEAMS, FR:] + product[BEAMS:, :FR]
        beams_refs[q][i, :, :FR] = real.astype(jnp.bfloat16)
        beams_refs[q][i, :, FR:] = imag.astype(jnp.bfloat16)

    def turn(q, group):
        part = pl.ds(pl.multiple_of(group * TILE, TILE), TILE)
        rows = beams_refs[q][:, part, :].reshape(256, 2 * FR)
        moved = jnp.dot(perm_ref[...], rows, preferred_element_type=jnp.float32)
        out_ref[part, q] = moved.reshape(TILE, TILE, 2 * FR).astype(jnp.bfloat16)

    groups = BEAMS // TILE
    for block in range(STATIONS // 128):
        weigh(0, 0, weight_a, block)
    for q in range(2):

        def pair(m, carry, q=q):
            for h, (now, later) in enumerate(((weight_a, weight_b), (weight_b, weight_a))):
                n = q * CHUNKS + 2 * m + h
                following = jnp.minimum(n + 1, 2 * CHUNKS - 1)
                for k in range(CHUNK):
                    multiply(q, 2 * m + h, k, now)
                    weigh(following // CHUNKS, following % CHUNKS, later, k)
                    if q == 1:
                        turn(0, 4 * (2 * m + h) + k)
            return carry

        lax.fori_loop(0, CHUNKS // 2, pair, 0)
    for group in range(groups):
        turn(1, group)


def form_beams(chan_start, gain_real, gain_imag, delays, received):
    whole = pl.BlockSpec(memory_space=pltpu.VMEM)
    phasor = pltpu.VMEM((2, BEAMS, STATIONS), jnp.float32)
    weight = pltpu.VMEM((CHUNK, 2 * BEAMS, STATIONS), jnp.bfloat16)
    return pl.pallas_call(
        beam_kernel,
        in_specs=[pl.BlockSpec(memory_space=pltpu.SMEM), whole, whole, whole, whole],
        out_specs=whole,
        out_shape=jax.ShapeDtypeStruct((BEAMS, 2, TILE, 2 * FR), jnp.bfloat16),
        scratch_shapes=[
            pltpu.VMEM((16, BEAMS, 2 * FR), jnp.bfloat16),
            pltpu.VMEM((16, BEAMS, 2 * FR), jnp.bfloat16),
            pltpu.VMEM((256, 256), jnp.bfloat16),
            weight,
            weight,
            phasor,
            phasor,
            phasor,
            phasor,
            pltpu.VMEM((BEAMS, STATIONS), jnp.float32),
            pltpu.VMEM((2, gain_real.shape[0], 1, STATIONS), jnp.float32),
        ],
        compiler_params=pltpu.CompilerParams(vmem_limit_bytes=BEAM_VMEM),
        name="beamform",
    )(chan_start, gain_real, gain_imag, delays, received.reshape(32, 16, 2, TILE, 2 * FR))


HALF = C // 2
ROWS = 64
LOCAL_BEAMS = 8


def transform(te_ref, to_ref, y_ref, beam, even_ref, odd_ref):
    even = y_ref[:, beam, 0].reshape(HALF, 2 * FR)
    odd = y_ref[:, beam, 1].reshape(HALF, 2 * FR)
    even_ref[...] = jnp.dot(te_ref[...], even, preferred_element_type=jnp.float32)
    odd_ref[...] = jnp.dot(to_ref[...], odd, preferred_element_type=jnp.float32)


def combine(taps_ref, beam, even_ref, odd_ref, pack_ref, signal_ref, out_ref):
    lane = lax.broadcasted_iota(jnp.int32, (ROWS, FR), 1)
    for r in range(0, HALF, ROWS):
        cos_rows, sin_rows = pl.ds(r, ROWS), pl.ds(HALF + r, ROWS)
        parts = []
        for ref in (even_ref, odd_ref):
            real = ref[cos_rows, :FR] - ref[sin_rows, FR:]
            imag = ref[sin_rows, :FR] + ref[cos_rows, FR:]
            parts.append((real, imag))
        for n1 in range(2):
            rows = pl.ds(n1 * HALF + r, ROWS)
            for ri in range(2):
                a, b = parts[0][ri], parts[1][ri]
                signal = a + b if n1 == 0 else a - b
                total = taps_ref[0, rows, :] * signal
                for k in range(1, TAPS):
                    shifted = jnp.where(lane >= k, pltpu.roll(signal, k, 1), 0.0)
                    total += taps_ref[k, rows, :] * shifted
                out_ref[beam, rows, ri * FR : (ri + 1) * FR] = total.astype(jnp.bfloat16)
                signal_ref[n1, cos_rows, ri * FR : (ri + 1) * FR] = signal.astype(jnp.bfloat16)
    source = lax.broadcasted_iota(jnp.int32, (2 * FR, FR), 0)
    target = lax.broadcasted_iota(jnp.int32, (2 * FR, FR), 1)
    frame, ri = source % FR - (FR - 4), source // FR
    for n1 in range(2):
        chosen = (frame >= 0) & (target == (beam * 4 + n1 * 2 + ri) * 4 + frame)
        pack_ref[...] += jnp.dot(
            signal_ref[n1],
            jnp.where(chosen, 1.0, 0.0).astype(jnp.bfloat16),
            preferred_element_type=jnp.float32,
        )


def synth_kernel(te_ref, to_ref, narrow_ref, y_ref, out_ref, tail_ref, *scratch):
    buffers, (pack_ref, taps_ref, signal_ref) = (scratch[0:2], scratch[2:4]), scratch[4:]
    step = pl.program_id(0)

    @pl.when(step == 0)
    def _():
        pack_ref[...] = jnp.zeros_like(pack_ref)
        narrow = narrow_ref[...]
        columns = jnp.transpose(jnp.concatenate([narrow, narrow], axis=0))
        for k in range(TAPS):
            taps_ref[k] = jnp.broadcast_to(columns[:, k : k + 1], (C, FR))

    last = pl.num_programs(0) - 1

    def half(i, back=True):
        transform(te_ref, to_ref, y_ref, 2 * step + i, *buffers[i])
        if back:
            combine(taps_ref, 2 * step + i - 1, *buffers[1 - i], pack_ref, signal_ref, out_ref)

    @pl.when(step == 0)
    def _():
        half(0, back=False)

    @pl.when((step > 0) & (step < last))
    def _():
        half(0)

    @pl.when(step < last)
    def _():
        half(1)

    @pl.when(step == last)
    def _():
        combine(taps_ref, LOCAL_BEAMS - 1, *buffers[1], pack_ref, signal_ref, out_ref)

    @pl.when(step == last)
    def _():
        lane = lax.broadcasted_iota(jnp.int32, (ROWS, FR), 1)
        for r in range(0, HALF, ROWS):
            rows = pl.ds(r, ROWS)
            packed = pack_ref[rows, :]
            total = jnp.zeros((ROWS, FR), jnp.float32)
            for k in range(1, TAPS):
                moved = jnp.where(lane % 4 < k, pltpu.roll(packed, FR - (4 - k), 1), 0.0)
                taps = jnp.where(
                    lane // 8 % 2 == 0, taps_ref[k, rows, :], taps_ref[k, pl.ds(HALF + r, ROWS), :]
                )
                total += taps * moved
            tail_ref[rows, :] = total.astype(jnp.bfloat16)


def synthesize(filter_taps, received):
    whole = pl.BlockSpec(memory_space=pltpu.VMEM)
    steps = LOCAL_BEAMS // 2 + 1
    product = pltpu.VMEM((C, 2 * FR), jnp.float32)
    return pl.pallas_call(
        synth_kernel,
        grid=(steps,),
        in_specs=[whole] * 4,
        out_specs=[whole, whole],
        out_shape=[
            jax.ShapeDtypeStruct((LOCAL_BEAMS, C, 2 * FR), jnp.bfloat16),
            jax.ShapeDtypeStruct((HALF, FR), jnp.bfloat16),
        ],
        scratch_shapes=[product] * 4
        + [
            pltpu.VMEM((HALF, FR), jnp.float32),
            pltpu.VMEM((TAPS, C, FR), jnp.float32),
            pltpu.VMEM((2, HALF, 2 * FR), jnp.bfloat16),
        ],
        compiler_params=pltpu.CompilerParams(vmem_limit_bytes=SYNTH_VMEM),
        name="synthesis",
    )(jnp.asarray(parity_table(0)), jnp.asarray(parity_table(1)), filter_taps, received)


PATCH_BEAMS = 4


def patch_kernel(in_ref, series_ref, out_ref):
    lane = lax.broadcasted_iota(jnp.int32, (FR, 2 * FR), 0)
    target = lax.broadcasted_iota(jnp.int32, (FR, 2 * FR), 1)
    frame, ri = target % FR, target // FR
    for i in range(PATCH_BEAMS):
        beam = pl.program_id(0) * PATCH_BEAMS + i
        for n1 in range(2):
            slot = beam * 4 + n1 * 2 + ri
            spread = jnp.where((frame < TAPS - 1) & (lane == slot * 4 + frame), 1.0, 0.0)
            rows = pl.ds(n1 * HALF, HALF)
            head = jnp.dot(
                in_ref[...], spread.astype(jnp.bfloat16), preferred_element_type=jnp.float32
            )
            out_ref[i, rows, :] = (series_ref[beam, rows, :].astype(jnp.float32) + head).astype(
                jnp.bfloat16
            )


def patch(incoming, series):
    whole = pl.BlockSpec(memory_space=pltpu.VMEM)
    return pl.pallas_call(
        patch_kernel,
        grid=(LOCAL_BEAMS // PATCH_BEAMS,),
        in_specs=[whole, whole],
        out_specs=pl.BlockSpec((PATCH_BEAMS, C, 2 * FR), lambda b: (b, 0, 0)),
        out_shape=jax.ShapeDtypeStruct((LOCAL_BEAMS, C, 2 * FR), jnp.bfloat16),
        compiler_params=pltpu.CompilerParams(vmem_limit_bytes=16 * 2**20),
        name="patch",
    )(incoming, series)


def per_device(voltages, exponents, gain_real, gain_imag, delays, filter_taps):
    local_count = gain_real.shape[1]
    chan_start = (lax.axis_index("chan") * local_count).astype(jnp.int32).reshape(1)
    turned = scale_and_turn(voltages, exponents.reshape(TILE, -1))
    turned, chan_start = lax.optimization_barrier((turned, chan_start))
    received = lax.all_to_all(turned, "chan", split_axis=0, concat_axis=0, tiled=True)
    beamed = form_beams(
        chan_start, jnp.transpose(gain_real), jnp.transpose(gain_imag), delays, received
    )
    spectra = lax.all_to_all(beamed, "chan", split_axis=0, concat_axis=0, tiled=True)
    series, tail = synthesize(filter_taps, spectra.reshape(32, LOCAL_BEAMS, 2, TILE, 2 * FR))
    groups = lax.axis_size("tm")
    incoming = lax.ppermute(tail, "tm", [(g, g + 1) for g in range(groups - 1)])
    return patch(incoming, series)


def solution(mesh):
    placed = (
        P("chan", None, "tm"),
        P("chan", None, "tm"),
        P(None, "chan"),
        P(None, "chan"),
        P(),
        P(),
    )
    return jax.shard_map(
        per_device, mesh=mesh, in_specs=placed, out_specs=P("chan", None, "tm"), check_vma=False
    )
```
